768 devices in a mesh: sub: 24 (over y_lo, z), blk: 32 (over y_hi, x, core).
Axes of the slice: x: 4, y: 8 (y_hi: 4, y_lo: 2; y = y_hi * 2 + y_lo), z: 12, core: 2. Of those that a mesh axis runs over, the one named last changes fastest.
Arguments:
- inv_factor: bfloat16 [768, 512, 512], P(('sub', 'blk')), may hold values from -0.25 to 0.25
- coupling: bfloat16 [768, 8, 512, 256], P(('sub', 'blk')), may hold values from -0.25 to 0.25
- batch_coupling: bfloat16 [768, 1, 16, 512], P(('sub', 'blk')), may hold values from -6 to 6
- tile_rows: int32 [768, 8], P(('sub', 'blk')), may hold values from 0 to 1535, as said below
- tile_count: int32 [768], P(('sub', 'blk')), may hold values from 6 to 8, as said below
- row_place: int32 [1536], replicated, may hold values from 0 to 1535, as said below
Outputs:
- schur_update: float32 [1536, 1, 16, 256], P(('sub', 'blk'))
The draws below stay inside these ranges and needn't reach their ends.
Inputs may be any that keep to these rules, and one draw needn't show every extreme that they name: `tile_rows`: the tiles of one group name distinct rows. With place = row_place[row], owner = place // 64 and block = (place % 64) // 2: at most 2 tiles of one group have one owner, at most 2 live tiles of all groups of one blk index have one owner and one block, and in every draw both bounds are reached. `tile_count`: padding tiles hold arbitrary values. `row_place`: A permutation of the block rows.
All inputs are finite; a program needn't handle non-finite values.
Results may differ from the reference program's by a relative error of at most 0.013.
Values may be sent and summed in bfloat16 or wider, within the bound.
A program may use at most 32 MiB of HBM per device.

```python
import jax
import jax.numpy as jnp
from jax import lax

NI = 512
IFW = 256
COLS = 16
NB = 1
NT = 8
RB_DEV = 2
CAP = 2
ROWS_OWN = 64
NROW = 1536
SUBDOMAINS = 768
N_SUB = 24
N_BLK = 32


def pattern(key):
    k_place, k_order, k_fav, k_shift, k_start = jax.random.split(jax.random.fold_in(key, 7), 5)
    row_place = jax.random.permutation(k_place, NROW).astype(jnp.int32)
    inverse = jnp.argsort(row_place).astype(jnp.int32)
    slots = N_SUB * CAP
    keys = jax.random.split(k_order, SUBDOMAINS)
    scores = jax.vmap(lambda k: jax.random.permutation(k, slots))(keys).astype(jnp.int32)
    favour = jax.random.randint(k_fav, (N_BLK,), 0, N_SUB).astype(jnp.int32)
    group_fav = jnp.tile(favour, N_SUB)
    slot_ids = jnp.arange(slots, dtype=jnp.int32)
    owner_of_slot = slot_ids // CAP
    forced = -CAP - 1 + slot_ids % CAP
    scores = jnp.where(owner_of_slot[None, :] == group_fav[:, None], forced[None, :], scores)
    order = jnp.argsort(scores, axis=1)[:, :NT].astype(jnp.int32)
    owner = order // CAP
    within = order % CAP
    group_ids = jnp.arange(SUBDOMAINS, dtype=jnp.int32)
    source_sub = group_ids // N_BLK
    source_blk = group_ids % N_BLK
    shift = jax.random.randint(k_shift, (N_BLK, N_SUB), 0, N_BLK).astype(jnp.int32)
    shift_owner = jnp.take_along_axis(shift[source_blk], owner, axis=1)
    block = (source_sub[:, None] + shift_owner) % N_BLK
    start = jax.random.randint(k_start, (SUBDOMAINS, N_SUB), 0, RB_DEV).astype(jnp.int32)
    start_owner = jnp.take_along_axis(start, owner, axis=1)
    local = block * RB_DEV + (start_owner + within) % RB_DEV
    place = owner * ROWS_OWN + local
    return (row_place, inverse[place].astype(jnp.int32))


def draw_tile_rows(key, part):
    return pattern(key)[1]


def draw_row_place(key, part):
    return pattern(key)[0]


def draw_tile_count(key, part):
    k_count, k_full = jax.random.split(jax.random.fold_in(key, 3))
    counts = jax.random.randint(k_count, (SUBDOMAINS,), 3 * NT // 4, NT + 1).astype(jnp.int32)
    full = jax.random.randint(k_full, (), 0, SUBDOMAINS).astype(jnp.int32)
    index = jnp.arange(SUBDOMAINS, dtype=jnp.int32)
    counts = jnp.where(index == full, NT, counts)
    counts = jnp.where(index == (full + 1) % SUBDOMAINS, 3 * NT // 4, counts)
    return counts.astype(jnp.int32)


def shard_levels(key, extent, pieces, least, top_value):
    factor_of, own = 1.0, jax.random.fold_in(key, 6)
    for axis_at, shards_of in pieces:
        draws = jnp.exp(jax.random.uniform(jax.random.fold_in(own, axis_at), (shards_of,), jnp.float32, least / len(pieces), top_value / len(pieces)))
        factor_of = factor_of * jnp.repeat(draws, extent[axis_at] // shards_of).reshape([-1 if axis == axis_at else 1 for axis in range(len(extent))])
    return factor_of


def gaussian(rng, dims, deviation, reach, cuts=(), held_as=jnp.bfloat16):
    loudness = shard_levels(rng, dims, cuts, -0.22, 0.18) if cuts else 1.0
    array = jax.random.normal(rng, dims, jnp.float32) * deviation * loudness
    return jnp.minimum(jnp.maximum(array, -reach), reach).astype(held_as)


def setup_inputs(seed: int = 0) -> dict:
    arg_keys = jax.random.split(jax.random.key(seed), 7)
    return {
        "inv_factor": gaussian(arg_keys[0], (SUBDOMAINS, NI, NI), NI ** -0.5, 0.25, ((0, 768),)),
        "coupling": gaussian(arg_keys[1], (SUBDOMAINS, NT, NI, IFW), NI ** -0.5, 0.25, ((0, 768),)),
        "batch_coupling": gaussian(arg_keys[2], (SUBDOMAINS, NB, COLS, NI), 1.0, 6.0, ((0, 768),)),
        "tile_rows": draw_tile_rows(jax.random.fold_in(arg_keys[6], 71), 0),
        "tile_count": draw_tile_count(jax.random.fold_in(arg_keys[6], 71), 0),
        "row_place": draw_row_place(jax.random.fold_in(arg_keys[6], 71), 0),
    }


def reference(inv_factor, coupling, batch_coupling, tile_rows, tile_count, row_place):
    def step(total, item):
        factor, tiles, columns, ids, count = item
        flat = columns.reshape(NB * COLS, NI)
        projected = jnp.dot(flat, factor.T, preferred_element_type=jnp.float32).astype(jnp.bfloat16)
        solved = jnp.dot(projected, factor, preferred_element_type=jnp.float32).astype(jnp.bfloat16)
        partial_value = jnp.einsum("cn,tnf->tcf", solved.astype(jnp.float32), tiles.astype(jnp.float32)).astype(jnp.bfloat16)
        live = jnp.arange(NT, dtype=jnp.int32) < count
        partial_value = jnp.where(live[:, None, None], partial_value.astype(jnp.float32), jnp.float32(0.0))
        partial_value = partial_value.reshape(NT, NB, COLS, IFW)
        total = total.at[row_place[ids]].add(partial_value)
        return total, None

    start = jnp.zeros((NROW, NB, COLS, IFW), jnp.float32)
    total, unused = lax.scan(step, start, (inv_factor, coupling, batch_coupling, tile_rows, tile_count))
    return -total
```

```python
import functools

import jax
import jax.numpy as jnp
from jax import lax
from jax.experimental import pallas as pl
from jax.experimental.pallas import tpu as pltpu
from jax.sharding import PartitionSpec as P

MESH = pl.DeviceIdType.MESH
BF16, F32, I32 = jnp.bfloat16, jnp.float32, jnp.int32
SLOTS = 2


def kernel(
    dims,
    rows_smem,
    count_smem,
    place_smem,
    factor_hbm,
    tiles_hbm,
    columns_hbm,
    out_ref,
    factor,
    tiles,
    columns,
    parts,
    pack,
    label_out,
    label_in,
    slots_out,
    slots_in,
    pick,
    total,
    sums_out,
    sums_in,
    load_sem,
    label_send,
    label_recv,
    slot_send,
    slot_recv,
    sum_send,
    sum_recv,
    ready,
):
    n_sub, n_blk, n_tiles, cols, rows_here = dims
    n_chip = n_blk // 2
    rows_owned = n_blk * rows_here
    half = n_sub // 2
    sub, blk = lax.axis_index("sub"), lax.axis_index("blk")
    chip, core = blk // 2, blk % 2
    collector = chip * 2 + 1
    barrier = pltpu.get_barrier_semaphore()

    loads = [
        pltpu.make_async_copy(src, dst, load_sem.at[i])
        for i, (src, dst) in enumerate(
            ((columns_hbm, columns), (factor_hbm, factor), (tiles_hbm, tiles))
        )
    ]
    for load in loads:
        load.start()

    @pl.when(core == 1)
    def _():
        def greet_column(i, carry):
            other = lax.rem(sub + i, n_sub)
            pl.semaphore_signal(
                barrier, inc=1, device_id={"sub": other, "blk": collector - 1}, device_id_type=MESH
            )

            @pl.when(i > 0)
            def _():
                pl.semaphore_signal(
                    barrier, inc=1, device_id={"sub": other, "blk": collector}, device_id_type=MESH
                )

            return carry

        lax.fori_loop(0, n_sub, greet_column, 0)

        def greet_plane(i, carry):
            other = lax.rem(chip + i, n_chip) * 2
            for c in range(2):
                pl.semaphore_signal(
                    barrier, inc=1, device_id={"sub": sub, "blk": other + c}, device_id_type=MESH
                )
            return carry

        lax.fori_loop(1, n_chip, greet_plane, 0)

    count = count_smem[0]
    owners, slot_of, local_of = [], [], []
    for t in range(n_tiles):
        row = jnp.clip(rows_smem[0, t], 0, place_smem.shape[0] - 1)
        place = place_smem[row]
        live = t < count
        owner = jnp.where(live, lax.shift_right_logical(place, rows_owned.bit_length() - 1), -1)
        rank = jnp.int32(0)
        for earlier in owners:
            rank = rank + jnp.where(earlier == owner, 1, 0)
        owners.append(owner)
        slot_of.append(jnp.where(live, owner * SLOTS + rank, -1))
        local_of.append(place & (rows_owned - 1))

    width = SLOTS * cols
    per_group = 128 // width
    lane = lax.broadcasted_iota(I32, (n_sub, 128), 1)
    to = lax.broadcasted_iota(I32, (n_sub, 128), 0)
    lane_slot = (lane // cols) % SLOTS
    mine = (lane // width) == lax.rem(sub, per_group)
    label = jnp.zeros((n_sub, 128), I32)
    for t in range(n_tiles):
        hit = mine & (to * SLOTS + lane_slot == slot_of[t])
        label = jnp.where(hit, local_of[t] * cols + lane % cols + 1, label)
    for o in range(n_sub):
        label_out[o] = label[o : o + 1]

    loads[0].wait()
    loads[1].wait()
    projected = lax.dot_general(
        columns[...], factor[...], (((1,), (1,)), ((), ())), preferred_element_type=F32
    ).astype(BF16)
    solved = jnp.dot(projected, factor[...], preferred_element_type=F32).astype(BF16)
    lane1 = lax.broadcasted_iota(I32, (1, 128), 1)
    target = jnp.full((1, 128), -1, I32)
    for t in range(n_tiles):
        at = jnp.where(slot_of[t] >= 0, slot_of[t] * cols, -1024)
        target = jnp.where(lane1 // cols == t, at + lane1 % cols, target)
    row_at = lax.broadcasted_iota(I32, (n_sub * width, 128), 0)
    pack[...] = jnp.where(row_at == target, 1.0, 0.0).astype(BF16)
    loads[2].wait()
    for t in range(n_tiles):
        parts[pl.ds(t * cols, cols)] = jnp.dot(
            solved, tiles[t], preferred_element_type=F32
        ).astype(BF16)
    slots_out[...] = jnp.dot(pack[...], parts[...], preferred_element_type=F32).astype(BF16)

    def slot_copy(dest):
        return pltpu.make_async_remote_copy(
            src_ref=slots_out.at[pl.ds(pl.multiple_of(dest * width, width), width)],
            dst_ref=slots_in.at[core, pl.ds(pl.multiple_of(sub * width, width), width)],
            send_sem=slot_send,
            recv_sem=slot_recv.at[core],
            device_id={"sub": dest, "blk": collector},
            device_id_type=MESH,
        )

    def label_copy(dest):
        return pltpu.make_async_remote_copy(
            src_ref=label_out.at[dest],
            dst_ref=label_in.at[core, sub],
            send_sem=label_send,
            recv_sem=label_recv.at[core],
            device_id={"sub": dest, "blk": collector},
            device_id_type=MESH,
        )

    def dest_of(i):
        k = i // 2
        dz = half // 2 + (1 - 2 * (k % 2)) * ((k + 1) // 2)
        z = lax.rem(sub + dz, half)
        y = (sub // half + 1 + i % 2) % 2
        return y * half + z

    @pl.when(core == 0)
    def _():
        pl.semaphore_wait(barrier, n_sub + n_chip - 1)

        def send(i, carry):
            dest = dest_of(i)
            label_copy(dest).start()
            slot_copy(dest).start()
            return carry

        lax.fori_loop(0, n_sub, send, 0)

        def say_ready(i, carry):
            pl.semaphore_signal(
                ready, inc=1, device_id={"sub": sub, "blk": i * 2 + 1}, device_id_type=MESH
            )
            return carry

        lax.fori_loop(0, n_chip, say_ready, 0)
        pltpu.make_async_copy(label_out, label_out, label_send).wait()
        pltpu.make_async_copy(slots_out, slots_out, slot_send).wait()
        pltpu.make_async_copy(sums_in, sums_in, sum_recv).wait()

    @pl.when(core == 1)
    def _():
        pl.semaphore_wait(barrier, n_sub + n_chip - 2)

        def send(i, carry):
            dest = dest_of(i)
            label_copy(dest).start()
            slot_copy(dest).start()
            return carry

        lax.fori_loop(0, n_sub - 1, send, 0)
        own = pl.ds(pl.multiple_of(sub * width, width), width)
        label_in[1, sub] = label_out[sub]
        slots_in[1, own] = slots_out[own]

        row_in = lax.broadcasted_iota(I32, (rows_owned * cols, 128), 0) + 1

        def add_core(c, sources):
            labels = label_in.at[c, pl.ds(0, sources)]
            pltpu.make_async_copy(labels, labels, label_recv.at[c]).wait()
            for g in range(n_sub // per_group):
                at = label_in[c, g * per_group]
                for s in range(1, per_group):
                    at = at + label_in[c, g * per_group + s]
                pick[:, pl.ds(g * 128, 128)] = jnp.where(row_in == at, 1.0, 0.0).astype(BF16)
            blocks = slots_in.at[c, pl.ds(0, sources * width)]
            pltpu.make_async_copy(blocks, blocks, slot_recv.at[c]).wait()
            return jnp.dot(pick[...], slots_in[c], preferred_element_type=F32)

        total[...] = add_core(1, n_sub - 1)
        sums_out[...] = (total[...] + add_core(0, n_sub)).astype(BF16)

        pl.semaphore_wait(ready, n_chip)
        rows = rows_here * cols

        def sum_copy(dest):
            return pltpu.make_async_remote_copy(
                src_ref=sums_out.at[pl.ds(pl.multiple_of(dest * rows, rows), rows)],
                dst_ref=sums_in.at[chip],
                send_sem=sum_send,
                recv_sem=sum_recv,
                device_id={"sub": sub, "blk": dest},
                device_id_type=MESH,
            )

        def send_sum(i, carry):
            sum_copy(lax.rem(blk + i, n_blk)).start()
            return carry

        lax.fori_loop(1, n_blk, send_sum, 0)
        sums_in[chip] = sums_out[pl.ds(pl.multiple_of(blk * rows, rows), rows)]
        labels = label_out.at[pl.ds(0, n_sub - 1)]
        pltpu.make_async_copy(labels, labels, label_send).wait()
        blocks = slots_out.at[pl.ds(0, (n_sub - 1) * width)]
        pltpu.make_async_copy(blocks, blocks, slot_send).wait()
        sums = sums_out.at[pl.ds(0, (n_blk - 1) * rows)]
        pltpu.make_async_copy(sums, sums, sum_send).wait()
        got = sums_in.at[pl.ds(0, n_chip - 1)]
        pltpu.make_async_copy(got, got, sum_recv).wait()

    acc = sums_in[0].astype(F32)
    for j in range(1, n_chip):
        acc = acc + sums_in[j].astype(F32)
    out_ref[...] = -acc


def on_device(inv_factor, coupling, batch_coupling, tile_rows, tile_count, row_place):
    n_sub, n_blk = lax.axis_size("sub"), lax.axis_size("blk")
    n_tiles, interior, width = coupling.shape[1:]
    cols = batch_coupling.shape[1] * batch_coupling.shape[2]
    rows_here = row_place.shape[0] // (n_sub * n_blk)
    dims = (n_sub, n_blk, n_tiles, cols, rows_here)
    rows_owned = rows_here * n_blk
    slot_rows = n_sub * SLOTS * cols
    smem = pl.BlockSpec(memory_space=pltpu.SMEM)
    hbm = pl.BlockSpec(memory_space=pl.ANY)
    dma = pltpu.SemaphoreType.DMA
    out = pl.pallas_call(
        functools.partial(kernel, dims),
        out_shape=jax.ShapeDtypeStruct((rows_here * cols, width), F32),
        in_specs=[smem, smem, smem, hbm, hbm, hbm],
        out_specs=pl.BlockSpec(memory_space=pltpu.VMEM),
        scratch_shapes=[
            pltpu.VMEM((interior, interior), BF16),
            pltpu.VMEM((n_tiles, interior, width), BF16),
            pltpu.VMEM((cols, interior), BF16),
            pltpu.VMEM((n_tiles * cols, width), BF16),
            pltpu.VMEM((slot_rows, n_tiles * cols), BF16),
            pltpu.VMEM((n_sub, 1, 128), I32),
            pltpu.VMEM((2, n_sub, 1, 128), I32),
            pltpu.VMEM((slot_rows, width), BF16),
            pltpu.VMEM((2, slot_rows, width), BF16),
            pltpu.VMEM((rows_owned * cols, slot_rows), BF16),
            pltpu.VMEM((rows_owned * cols, width), F32),
            pltpu.VMEM((rows_owned * cols, width), BF16),
            pltpu.VMEM((n_blk // 2, rows_here * cols, width), BF16),
            dma((3,)),
            dma,
            dma((2,)),
            dma,
            dma((2,)),
            dma,
            dma,
            pltpu.SemaphoreType.REGULAR,
        ],
        compiler_params=pltpu.CompilerParams(
            collective_id=0, has_side_effects=True, vmem_limit_bytes=24 * 1024 * 1024
        ),
    )(
        tile_rows,
        tile_count,
        row_place,
        inv_factor[0],
        coupling[0],
        batch_coupling.reshape(cols, interior),
    )
    return out.reshape(rows_here, batch_coupling.shape[1], batch_coupling.shape[2], width)


def solution(mesh):
    return jax.shard_map(
        on_device,
        mesh=mesh,
        in_specs=(
            P(("sub", "blk"), None, None),
            P(("sub", "blk"), None, None, None),
            P(("sub", "blk"), None, None, None),
            P(("sub", "blk"), None),
            P(("sub", "blk")),
            P(),
        ),
        out_specs=P(("sub", "blk"), None, None, None),
        check_vma=False,
    )
```

```python
import functools

import jax
import jax.numpy as jnp
from jax import lax
from jax.experimental import pallas as pl
from jax.experimental.pallas import tpu as pltpu
from jax.sharding import PartitionSpec as P

MESH = pl.DeviceIdType.MESH
BF16, F32, I32 = jnp.bfloat16, jnp.float32, jnp.int32
SLOTS = 2
LANES = 128


def kernel(
    dims,
    rows_hbm,
    count_hbm,
    place_hbm,
    factor_hbm,
    tiles_hbm,
    columns_hbm,
    out_ref,
    rows_smem,
    count_smem,
    place_smem,
    factor,
    tiles,
    columns,
    parts,
    label_out,
    label_in,
    slots_out,
    slots_in,
    pick,
    sums_out,
    sums_in,
    load_sem,
    label_send,
    label_recv,
    slot_send,
    slot_recv,
    sum_send,
    sum_recv,
):
    n_sub, n_blk, n_tiles, cols, rows_here = dims
    n_chip, n_src, c8 = n_blk // 2, n_sub * 2, cols // 2
    rows_owned = n_blk * rows_here
    half = n_sub // 2
    sub, blk = lax.axis_index("sub"), lax.axis_index("blk")
    chip, core = blk // 2, blk % 2
    barrier = pltpu.get_barrier_semaphore()

    loads = [
        pltpu.make_async_copy(src, dst, load_sem.at[i])
        for i, (src, dst) in enumerate(
            (
                (rows_hbm, rows_smem),
                (count_hbm, count_smem),
                (place_hbm, place_smem),
                (columns_hbm, columns),
                (factor_hbm, factor),
                (tiles_hbm, tiles),
            )
        )
    ]
    for load in loads:
        load.start()

    def greet(dev_sub, dev_blk):
        pl.semaphore_signal(
            barrier, inc=1, device_id={"sub": dev_sub, "blk": dev_blk}, device_id_type=MESH
        )

    def greet_column(i, carry):
        other = lax.rem(sub + i, n_sub)
        greet(other, chip * 2)
        greet(other, chip * 2 + 1)
        return carry

    def greet_plane(i, carry):
        other = lax.rem(chip + i, n_chip) * 2
        greet(sub, other)
        greet(sub, other + 1)
        return carry

    lax.fori_loop(1, n_sub, greet_column, 0)
    greet(sub, blk + 1 - 2 * core)
    lax.fori_loop(1, n_chip, greet_plane, 0)

    for load in loads[:3]:
        load.wait()

    count = count_smem[0]
    owners, slot_of, local_of = [], [], []
    for t in range(n_tiles):
        row = jnp.clip(rows_smem[0, t], 0, place_smem.shape[0] - 1)
        place = place_smem[row]
        live = t < count
        owner = jnp.where(live, lax.shift_right_logical(place, rows_owned.bit_length() - 1), -1)
        rank = jnp.int32(0)
        for earlier in owners:
            rank = rank + jnp.where(earlier == owner, 1, 0)
        owners.append(owner)
        slot_of.append(jnp.where(live, owner * SLOTS + rank, -1024))
        local_of.append(place & (rows_owned - 1))

    width = SLOTS * c8
    per_group = LANES // width
    lane = lax.broadcasted_iota(I32, (n_sub, LANES), 1)
    to = lax.broadcasted_iota(I32, (n_sub, LANES), 0)
    lane_slot = (lane // c8) % SLOTS
    mine = (lane // width) == lax.rem(sub, per_group)
    label = jnp.zeros((n_sub, LANES), I32)
    for t in range(n_tiles):
        hit = mine & (to * SLOTS + lane_slot == slot_of[t])
        label = jnp.where(hit, local_of[t] * c8 + lane % c8 + 1, label)
    for o in range(n_sub):
        label_out[o] = label[o : o + 1]

    loads[3].wait()
    loads[4].wait()
    projected = lax.dot_general(
        columns[...], factor[...], (((1,), (1,)), ((), ())), preferred_element_type=F32
    ).astype(BF16)
    solved = jnp.dot(projected, factor[...], preferred_element_type=F32).astype(BF16)
    in_lane = lax.broadcasted_iota(I32, (1, n_tiles * c8), 1)
    target = jnp.full((1, n_tiles * c8), -1, I32)
    for t in range(n_tiles):
        target = jnp.where(in_lane // c8 == t, slot_of[t] * c8 + in_lane % c8, target)
    row_at = lax.broadcasted_iota(I32, (n_sub * width, n_tiles * c8), 0)
    pack = jnp.where(row_at == target, 1.0, 0.0).astype(BF16)
    loads[5].wait()
    for t in range(0, n_tiles, 2):
        pair = [
            jnp.dot(solved, tiles[u], preferred_element_type=F32) for u in (t, t + 1)
        ]
        for h in range(2):
            for c in range(2):
                cut = [p[c * c8 : (c + 1) * c8, h * LANES : (h + 1) * LANES] for p in pair]
                parts[pl.ds(t * c8, 2 * c8), pl.ds((h * 2 + c) * LANES, LANES)] = (
                    jnp.concatenate(cut, axis=0).astype(BF16)
                )
    for h in range(2):
        slots_out[h] = jnp.dot(
            pack, parts[:, pl.ds(h * 2 * LANES, 2 * LANES)], preferred_element_type=F32
        ).astype(BF16)

    source = core * n_sub + sub

    def slot_copy(dest, h):
        return pltpu.make_async_remote_copy(
            src_ref=slots_out.at[h, pl.ds(pl.multiple_of(dest * width, width), width)],
            dst_ref=slots_in.at[pl.ds(pl.multiple_of(source * width, width), width)],
            send_sem=slot_send,
            recv_sem=slot_recv,
            device_id={"sub": dest, "blk": chip * 2 + h},
            device_id_type=MESH,
        )

    def label_copy(dest, h):
        return pltpu.make_async_remote_copy(
            src_ref=label_out.at[dest],
            dst_ref=label_in.at[source],
            send_sem=label_send,
            recv_sem=label_recv,
            device_id={"sub": dest, "blk": chip * 2 + h},
            device_id_type=MESH,
        )

    def dest_of(i):
        k = i // 2
        dz = half // 2 + (1 - 2 * (k % 2)) * ((k + 1) // 2)
        z = lax.rem(sub + dz, half)
        y = (sub // half + 1 + i % 2) % 2
        return y * half + z

    pl.semaphore_wait(barrier, n_src - 1 + n_blk - 2)
    for h in range(2):

        def send_labels(i, carry, h=h):
            label_copy(dest_of(i), h).start()
            return carry

        def send_slots(i, carry, h=h):
            slot_copy(dest_of(i), h).start()
            return carry

        lax.fori_loop(0, n_sub - 1, send_labels, 0)
        lax.fori_loop(0, n_sub - 1, send_slots, 0)

        @pl.when(core != h)
        def _(h=h):
            label_copy(sub, h).start()
            slot_copy(sub, h).start()

        @pl.when(core == h)
        def _(h=h):
            label_in[source] = label_out[sub]
            slots_in[pl.ds(pl.multiple_of(source * width, width), width)] = slots_out[
                h, pl.ds(pl.multiple_of(sub * width, width), width)
            ]

    labels = label_in.at[pl.ds(0, n_src - 1)]
    pltpu.make_async_copy(labels, labels, label_recv).wait()
    row_in = lax.broadcasted_iota(I32, (rows_owned * c8, LANES), 0) + 1
    for g in range(n_src // per_group):
        at = label_in[g * per_group]
        for s in range(1, per_group):
            at = at + label_in[g * per_group + s]
        pick[:, pl.ds(g * LANES, LANES)] = jnp.where(row_in == at, 1.0, 0.0).astype(BF16)
    blocks = slots_in.at[pl.ds(0, (n_src - 1) * width)]
    pltpu.make_async_copy(blocks, blocks, slot_recv).wait()
    sums_out[...] = jnp.dot(pick[...], slots_in[...], preferred_element_type=F32).astype(BF16)

    rows = rows_here * c8

    def send_sum(i, carry):
        dest = lax.rem(blk + i, n_blk)
        pltpu.make_async_remote_copy(
            src_ref=sums_out.at[pl.ds(pl.multiple_of(dest * rows, rows), rows)],
            dst_ref=sums_in.at[core, chip],
            send_sem=sum_send,
            recv_sem=sum_recv,
            device_id={"sub": sub, "blk": dest},
            device_id_type=MESH,
        ).start()
        return carry

    lax.fori_loop(1, n_blk, send_sum, 0)
    sums_in[core, chip] = sums_out[pl.ds(pl.multiple_of(blk * rows, rows), rows)]
    pltpu.make_async_copy(labels, labels, label_send).wait()
    pltpu.make_async_copy(blocks, blocks, slot_send).wait()
    sums = sums_out.at[pl.ds(0, (n_blk - 1) * rows)]
    pltpu.make_async_copy(sums, sums, sum_send).wait()
    pltpu.make_async_copy(sums, sums, sum_recv).wait()

    for h in range(2):
        acc = sums_in[h, 0].astype(F32)
        for j in range(1, n_chip):
            acc = acc + sums_in[h, j].astype(F32)
        for r in range(rows_here):
            for c in range(2):
                out_ref[pl.ds((r * 2 + c) * c8, c8), pl.ds(h * LANES, LANES)] = -acc[
                    r * c8 : (r + 1) * c8, c * LANES : (c + 1) * LANES
                ]


def on_device(inv_factor, coupling, batch_coupling, tile_rows, tile_count, row_place):
    n_sub, n_blk = lax.axis_size("sub"), lax.axis_size("blk")
    n_tiles, interior, dofs = coupling.shape[1:]
    cols = batch_coupling.shape[1] * batch_coupling.shape[2]
    c8 = cols // 2
    rows_here = row_place.shape[0] // (n_sub * n_blk)
    dims = (n_sub, n_blk, n_tiles, cols, rows_here)
    rows_owned = rows_here * n_blk
    slot_rows = n_sub * SLOTS * c8
    hbm = pl.BlockSpec(memory_space=pltpu.HBM)
    dma = pltpu.SemaphoreType.DMA
    out = pl.pallas_call(
        functools.partial(kernel, dims),
        out_shape=jax.ShapeDtypeStruct((rows_here * cols, dofs), F32),
        in_specs=[hbm] * 6,
        out_specs=pl.BlockSpec(memory_space=pltpu.VMEM),
        scratch_shapes=[
            pltpu.SMEM(tile_rows.shape, I32),
            pltpu.SMEM(tile_count.shape, I32),
            pltpu.SMEM(row_place.shape, I32),
            pltpu.VMEM((interior, interior), BF16),
            pltpu.VMEM((n_tiles, interior, dofs), BF16),
            pltpu.VMEM((cols, interior), BF16),
            pltpu.VMEM((n_tiles * c8, 2 * dofs), BF16),
            pltpu.VMEM((n_sub, 1, LANES), I32),
            pltpu.VMEM((2 * n_sub, 1, LANES), I32),
            pltpu.VMEM((2, slot_rows, dofs), BF16),
            pltpu.VMEM((2 * slot_rows, dofs), BF16),
            pltpu.VMEM((rows_owned * c8, 2 * slot_rows), BF16),
            pltpu.VMEM((rows_owned * c8, dofs), BF16),
            pltpu.VMEM((2, n_blk // 2, rows_here * c8, dofs), BF16),
            dma((6,)),
            dma,
            dma,
            dma,
            dma,
            dma,
            dma,
        ],
        compiler_params=pltpu.CompilerParams(
            collective_id=0, has_side_effects=True, vmem_limit_bytes=60 * 1024 * 1024
        ),
    )(
        tile_rows,
        tile_count,
        row_place,
        inv_factor[0],
        coupling[0],
        batch_coupling.reshape(cols, interior),
    )
    return out.reshape(rows_here, batch_coupling.shape[1], batch_coupling.shape[2], dofs)


def solution(mesh):
    return jax.shard_map(
        on_device,
        mesh=mesh,
        in_specs=(
            P(("sub", "blk"), None, None),
            P(("sub", "blk"), None, None, None),
            P(("sub", "blk"), None, None, None),
            P(("sub", "blk"), None),
            P(("sub", "blk")),
            P(),
        ),
        out_specs=P(("sub", "blk"), None, None, None),
        check_vma=False,
    )
```

```python
import functools

import jax
import jax.numpy as jnp
from jax import lax
from jax.experimental import pallas as pl
from jax.experimental.pallas import tpu as pltpu
from jax.sharding import PartitionSpec as P

MESH = pl.DeviceIdType.MESH
BF16, F32, I32 = jnp.bfloat16, jnp.float32, jnp.int32
SLOTS = 2
LANES = 128
LEAD = 24
PLANE = [(2, x) for x in (2, 1, 3, 0)]
PLANE += [(y, x) for x in (2, 1, 3, 0) for y in (1, 3)] + [(0, x) for x in (2, 1, 3)]


def kernel(
    dims,
    rows_hbm,
    count_hbm,
    place_hbm,
    factor_hbm,
    tiles_hbm,
    columns_hbm,
    out_ref,
    rows_smem,
    count_smem,
    place_smem,
    factor,
    tiles,
    columns,
    parts,
    label_out,
    label_in,
    slots_out,
    slots_in,
    pick,
    sums_out,
    sums_in,
    load_sem,
    label_send,
    label_recv,
    pair_send,
    pair_recv,
    slot_send,
    slot_recv,
    sum_send,
    sum_recv,
):
    n_sub, n_blk, n_tiles, cols, rows_here = dims
    n_chip, n_src, c8 = n_blk // 2, n_sub * 2, cols // 2
    rows_owned = n_blk * rows_here
    half = n_sub // 2
    sub, blk = lax.axis_index("sub"), lax.axis_index("blk")
    chip, core = blk // 2, blk % 2
    barrier = pltpu.get_barrier_semaphore()

    loads = [
        pltpu.make_async_copy(src, dst, load_sem.at[i])
        for i, (src, dst) in enumerate(
            (
                (rows_hbm, rows_smem),
                (count_hbm, count_smem),
                (place_hbm, place_smem),
                (columns_hbm, columns),
                (factor_hbm, factor),
                (tiles_hbm, tiles),
            )
        )
    ]
    for load in loads:
        load.start()

    def greet(dev_sub, dev_blk):
        pl.semaphore_signal(
            barrier, inc=1, device_id={"sub": dev_sub, "blk": dev_blk}, device_id_type=MESH
        )

    y, z = sub // half, lax.rem(sub, half)
    column = []
    for k in range(half):
        at = z + half // 2 + (1 - 2 * (k % 2)) * ((k + 1) // 2)
        at = jnp.where(at >= half, at - half, at)
        column += [(1 - y) * half + at, y * half + at]
    plane = []
    for dy, dx in PLANE:
        plane.append((((chip // 4 + dy) % 4) * 4 + (chip + dx) % 4) * 2)

    for other in column[:-1]:
        greet(other, chip * 2)
        greet(other, chip * 2 + 1)
    greet(sub, blk + 1 - 2 * core)
    for other in plane:
        greet(sub, other)
        greet(sub, other + 1)

    for load in loads[:3]:
        load.wait()

    count = count_smem[0]
    owners, slot_of, local_of = [], [], []
    for t in range(n_tiles):
        row = jnp.clip(rows_smem[0, t], 0, place_smem.shape[0] - 1)
        place = place_smem[row]
        live = t < count
        owner = jnp.where(live, lax.shift_right_logical(place, rows_owned.bit_length() - 1), -1)
        rank = jnp.int32(0)
        for earlier in owners:
            rank = rank + jnp.where(earlier == owner, 1, 0)
        owners.append(owner)
        slot_of.append(jnp.where(live, owner * SLOTS + rank, -1024))
        local_of.append(place & (rows_owned - 1))

    width = SLOTS * c8
    per_group = LANES // width
    lane = lax.broadcasted_iota(I32, (n_sub, LANES), 1)
    to = lax.broadcasted_iota(I32, (n_sub, LANES), 0)
    lane_slot = (lane // c8) % SLOTS
    mine = (lane // width) == lax.rem(sub, per_group)
    label = jnp.zeros((n_sub, LANES), I32)
    for t in range(n_tiles):
        hit = mine & (to * SLOTS + lane_slot == slot_of[t])
        label = jnp.where(hit, local_of[t] * c8 + lane % c8 + 1, label)
    for o in range(n_sub):
        label_out[o] = label[o : o + 1]

    loads[3].wait()
    loads[4].wait()
    projected = lax.dot_general(
        columns[...], factor[...], (((1,), (1,)), ((), ())), preferred_element_type=F32
    ).astype(BF16)
    solved = jnp.dot(projected, factor[...], preferred_element_type=F32).astype(BF16)
    in_lane = lax.broadcasted_iota(I32, (1, n_tiles * c8), 1)
    target = jnp.full((1, n_tiles * c8), -1, I32)
    for t in range(n_tiles):
        target = jnp.where(in_lane // c8 == t, slot_of[t] * c8 + in_lane % c8, target)
    row_at = lax.broadcasted_iota(I32, (n_sub * width, n_tiles * c8), 0)
    pack = jnp.where(row_at == target, 1.0, 0.0).astype(BF16)
    loads[5].wait()
    for t in range(0, n_tiles, 2):
        pair = [
            jnp.dot(solved, tiles[u], preferred_element_type=F32) for u in (t, t + 1)
        ]
        for h in range(2):
            for c in range(2):
                cut = [p[c * c8 : (c + 1) * c8, h * LANES : (h + 1) * LANES] for p in pair]
                parts[pl.ds(t * c8, 2 * c8), pl.ds((h * 2 + c) * LANES, LANES)] = (
                    jnp.concatenate(cut, axis=0).astype(BF16)
                )
    for h in range(2):
        slots_out[h] = jnp.dot(
            pack, parts[:, pl.ds(h * 2 * LANES, 2 * LANES)], preferred_element_type=F32
        ).astype(BF16)

    source = core * n_sub + sub

    def slot_copy(dest, h):
        return pltpu.make_async_remote_copy(
            src_ref=slots_out.at[h, pl.ds(pl.multiple_of(dest * width, width), width)],
            dst_ref=slots_in.at[pl.ds(pl.multiple_of(source * width, width), width)],
            send_sem=slot_send,
            recv_sem=slot_recv,
            device_id={"sub": dest, "blk": chip * 2 + h},
            device_id_type=MESH,
        )

    def label_copy(dest):
        return pltpu.make_async_remote_copy(
            src_ref=label_out.at[dest],
            dst_ref=label_in.at[source],
            send_sem=label_send,
            recv_sem=label_recv,
            device_id={"sub": dest, "blk": blk},
            device_id_type=MESH,
        )

    pl.semaphore_wait(barrier, n_src - 1 + n_blk - 2)
    for dest in column[:-1]:
        label_copy(dest).start()
    label_in[source] = label_out[sub]
    order = [(k - shift, h, k) for h, shift in ((0, LEAD), (1, 0)) for k in range(n_sub)]
    for _, h, k in sorted(order):
        if k < n_sub - 1:
            slot_copy(column[k], h).start()
        else:

            @pl.when(core != h)
            def _(h=h):
                slot_copy(sub, h).start()

            @pl.when(core == h)
            def _(h=h):
                slots_in[pl.ds(pl.multiple_of(source * width, width), width)] = slots_out[
                    h, pl.ds(pl.multiple_of(sub * width, width), width)
                ]

    labels = label_in.at[pl.ds(0, n_sub - 1)]
    pltpu.make_async_copy(labels, labels, label_recv).wait()
    mine = label_in.at[pl.ds(core * n_sub, n_sub)]
    pair = pltpu.make_async_remote_copy(
        src_ref=mine,
        dst_ref=mine,
        send_sem=pair_send,
        recv_sem=pair_recv,
        device_id={"sub": sub, "blk": blk + 1 - 2 * core},
        device_id_type=MESH,
    )
    pair.start()
    pair.wait_recv()
    row_in = lax.broadcasted_iota(I32, (rows_owned * c8, LANES), 0) + 1
    for g in range(n_src // per_group):
        at = label_in[g * per_group]
        for s in range(1, per_group):
            at = at + label_in[g * per_group + s]
        pick[:, pl.ds(g * LANES, LANES)] = jnp.where(row_in == at, 1.0, 0.0).astype(BF16)
    blocks = slots_in.at[pl.ds(0, (n_src - 1) * width)]
    pltpu.make_async_copy(blocks, blocks, slot_recv).wait()
    sums_out[...] = jnp.dot(pick[...], slots_in[...], preferred_element_type=F32).astype(BF16)

    rows = rows_here * c8

    def send_sum(dest):
        pltpu.make_async_remote_copy(
            src_ref=sums_out.at[pl.ds(pl.multiple_of(dest * rows, rows), rows)],
            dst_ref=sums_in.at[core, chip],
            send_sem=sum_send,
            recv_sem=sum_recv.at[core],
            device_id={"sub": sub, "blk": dest},
            device_id_type=MESH,
        ).start()

    send_sum(blk + 1 - 2 * core)
    for other in plane:
        send_sum(other)
        send_sum(other + 1)
    keep = pltpu.make_async_copy(
        sums_out.at[pl.ds(pl.multiple_of(blk * rows, rows), rows)],
        sums_in.at[core, chip],
        sum_recv.at[core],
    )
    keep.start()
    pltpu.make_async_copy(labels, labels, label_send).wait()
    pltpu.make_async_copy(blocks, blocks, slot_send).wait()
    sums = sums_out.at[pl.ds(0, (n_blk - 1) * rows)]
    pltpu.make_async_copy(sums, sums, sum_send).wait()
    pair.wait_send()

    for h in range(2):
        pltpu.make_async_copy(sums_in.at[h], sums_in.at[h], sum_recv.at[h]).wait()
        acc = sums_in[h, 0].astype(F32)
        for j in range(1, n_chip):
            acc = acc + sums_in[h, j].astype(F32)
        for r in range(rows_here):
            for c in range(2):
                out_ref[pl.ds((r * 2 + c) * c8, c8), pl.ds(h * LANES, LANES)] = -acc[
                    r * c8 : (r + 1) * c8, c * LANES : (c + 1) * LANES
                ]


def on_device(inv_factor, coupling, batch_coupling, tile_rows, tile_count, row_place):
    n_sub, n_blk = lax.axis_size("sub"), lax.axis_size("blk")
    n_tiles, interior, dofs = coupling.shape[1:]
    cols = batch_coupling.shape[1] * batch_coupling.shape[2]
    c8 = cols // 2
    rows_here = row_place.shape[0] // (n_sub * n_blk)
    dims = (n_sub, n_blk, n_tiles, cols, rows_here)
    rows_owned = rows_here * n_blk
    slot_rows = n_sub * SLOTS * c8
    hbm = pl.BlockSpec(memory_space=pltpu.HBM)
    dma = pltpu.SemaphoreType.DMA
    out = pl.pallas_call(
        functools.partial(kernel, dims),
        out_shape=jax.ShapeDtypeStruct((rows_here * cols, dofs), F32),
        in_specs=[hbm] * 6,
        out_specs=pl.BlockSpec(memory_space=pltpu.VMEM),
        scratch_shapes=[
            pltpu.SMEM(tile_rows.shape, I32),
            pltpu.SMEM(tile_count.shape, I32),
            pltpu.SMEM(row_place.shape, I32),
            pltpu.VMEM((interior, interior), BF16),
            pltpu.VMEM((n_tiles, interior, dofs), BF16),
            pltpu.VMEM((cols, interior), BF16),
            pltpu.VMEM((n_tiles * c8, 2 * dofs), BF16),
            pltpu.VMEM((n_sub, 1, LANES), I32),
            pltpu.VMEM((2 * n_sub, 1, LANES), I32),
            pltpu.VMEM((2, slot_rows, dofs), BF16),
            pltpu.VMEM((2 * slot_rows, dofs), BF16),
            pltpu.VMEM((rows_owned * c8, 2 * slot_rows), BF16),
            pltpu.VMEM((rows_owned * c8, dofs), BF16),
            pltpu.VMEM((2, n_blk // 2, rows_here * c8, dofs), BF16),
            dma((6,)),
            dma,
            dma,
            dma,
            dma,
            dma,
            dma,
            dma,
            dma((2,)),
        ],
        compiler_params=pltpu.CompilerParams(
            collective_id=0, has_side_effects=True, vmem_limit_bytes=60 * 1024 * 1024
        ),
    )(
        tile_rows,
        tile_count,
        row_place,
        inv_factor[0],
        coupling[0],
        batch_coupling.reshape(cols, interior),
    )
    return out.reshape(rows_here, batch_coupling.shape[1], batch_coupling.shape[2], dofs)


def solution(mesh):
    return jax.shard_map(
        on_device,
        mesh=mesh,
        in_specs=(
            P(("sub", "blk"), None, None),
            P(("sub", "blk"), None, None, None),
            P(("sub", "blk"), None, None, None),
            P(("sub", "blk"), None),
            P(("sub", "blk")),
            P(),
        ),
        out_specs=P(("sub", "blk"), None, None, None),
        check_vma=False,
    )
```

```python
import functools

import jax
import jax.numpy as jnp
from jax import lax
from jax.experimental import pallas as pl
from jax.experimental.pallas import tpu as pltpu
from jax.sharding import PartitionSpec as P

MESH = pl.DeviceIdType.MESH
BF16, F32, I32 = jnp.bfloat16, jnp.float32, jnp.int32
SLOTS = 2
LANES = 128
PLANE = [(2, x) for x in (2, 1, 3, 0)]
PLANE += [(y, x) for x in (2, 1, 3, 0) for y in (1, 3)] + [(0, x) for x in (2, 1, 3)]


def kernel(
    dims,
    rows_hbm,
    count_hbm,
    place_hbm,
    factor_hbm,
    tiles_hbm,
    columns_hbm,
    out_ref,
    rows_smem,
    count_smem,
    place_smem,
    factor,
    tiles,
    columns,
    parts,
    label_out,
    label_in,
    slots_out,
    slots_in,
    pick,
    sums_out,
    sums_in,
    load_sem,
    label_send,
    label_recv,
    pair_send,
    pair_recv,
    slot_send,
    slot_recv,
    sum_send,
    sum_recv,
):
    n_sub, n_blk, n_tiles, cols, rows_here = dims
    n_chip, n_src, c8 = n_blk // 2, n_sub * 2, cols // 2
    rows_owned = n_blk * rows_here
    half = n_sub // 2
    sub, blk = lax.axis_index("sub"), lax.axis_index("blk")
    chip, core = blk // 2, blk % 2
    barrier = pltpu.get_barrier_semaphore()

    loads = [
        pltpu.make_async_copy(src, dst, load_sem.at[i])
        for i, (src, dst) in enumerate(
            (
                (rows_hbm, rows_smem),
                (count_hbm, count_smem),
                (place_hbm, place_smem),
                (columns_hbm, columns),
                (factor_hbm, factor),
                (tiles_hbm, tiles),
            )
        )
    ]

    def greet(dev_sub, dev_blk):
        pl.semaphore_signal(
            barrier, inc=1, device_id={"sub": dev_sub, "blk": dev_blk}, device_id_type=MESH
        )

    y, z = sub // half, lax.rem(sub, half)
    column = []
    for k in range(half):
        at = z + half // 2 + (1 - 2 * (k % 2)) * ((k + 1) // 2)
        at = jnp.where(at >= half, at - half, at)
        column += [(1 - y) * half + at, y * half + at]
    plane = []
    for dy, dx in PLANE:
        plane.append((((chip // 4 + dy) % 4) * 4 + (chip + dx) % 4) * 2)

    for other in column[:-1]:
        greet(other, chip * 2)
        greet(other, chip * 2 + 1)
    for load in loads:
        load.start()
    greet(sub, blk + 1 - 2 * core)
    for other in plane:
        greet(sub, other)
        greet(sub, other + 1)

    for load in loads[:3]:
        load.wait()

    count = count_smem[0]
    owners, slot_of, local_of = [], [], []
    for t in range(n_tiles):
        row = jnp.clip(rows_smem[0, t], 0, place_smem.shape[0] - 1)
        place = place_smem[row]
        live = t < count
        owner = jnp.where(live, lax.shift_right_logical(place, rows_owned.bit_length() - 1), -1)
        rank = jnp.int32(0)
        for earlier in owners:
            rank = rank + jnp.where(earlier == owner, 1, 0)
        owners.append(owner)
        slot_of.append(jnp.where(live, owner * SLOTS + rank, -1024))
        local_of.append(place & (rows_owned - 1))

    width = SLOTS * c8
    per_group = LANES // width
    lane = lax.broadcasted_iota(I32, (n_sub, LANES), 1)
    to = lax.broadcasted_iota(I32, (n_sub, LANES), 0)
    lane_slot = (lane // c8) % SLOTS
    mine = (lane // width) == lax.rem(sub, per_group)
    label = jnp.zeros((n_sub, LANES), I32)
    for t in range(n_tiles):
        hit = mine & (to * SLOTS + lane_slot == slot_of[t])
        label = jnp.where(hit, local_of[t] * c8 + lane % c8 + 1, label)
    for o in range(n_sub):
        label_out[o] = label[o : o + 1]

    loads[3].wait()
    loads[4].wait()
    projected = lax.dot_general(
        columns[...], factor[...], (((1,), (1,)), ((), ())), preferred_element_type=F32
    ).astype(BF16)
    solved = jnp.dot(projected, factor[...], preferred_element_type=F32).astype(BF16)
    in_lane = lax.broadcasted_iota(I32, (1, n_tiles * c8), 1)
    target = jnp.full((1, n_tiles * c8), -1, I32)
    for t in range(n_tiles):
        target = jnp.where(in_lane // c8 == t, slot_of[t] * c8 + in_lane % c8, target)
    row_at = lax.broadcasted_iota(I32, (n_sub * width, n_tiles * c8), 0)
    pack = jnp.where(row_at == target, 1.0, 0.0).astype(BF16)
    loads[5].wait()
    for t in range(0, n_tiles, 2):
        pair = [
            jnp.dot(solved, tiles[u], preferred_element_type=F32) for u in (t, t + 1)
        ]
        for h in range(2):
            for c in range(2):
                cut = [p[c * c8 : (c + 1) * c8, h * LANES : (h + 1) * LANES] for p in pair]
                parts[pl.ds(t * c8, 2 * c8), pl.ds((h * 2 + c) * LANES, LANES)] = (
                    jnp.concatenate(cut, axis=0).astype(BF16)
                )

    def fill_slots(h):
        slots_out[h] = jnp.dot(
            pack, parts[:, pl.ds(h * 2 * LANES, 2 * LANES)], preferred_element_type=F32
        ).astype(BF16)

    fill_slots(0)

    source = core * n_sub + sub

    def slot_copy(dest, h):
        return pltpu.make_async_remote_copy(
            src_ref=slots_out.at[h, pl.ds(pl.multiple_of(dest * width, width), width)],
            dst_ref=slots_in.at[pl.ds(pl.multiple_of(source * width, width), width)],
            send_sem=slot_send,
            recv_sem=slot_recv,
            device_id={"sub": dest, "blk": chip * 2 + h},
            device_id_type=MESH,
        )

    def label_copy(dest):
        return pltpu.make_async_remote_copy(
            src_ref=label_out.at[dest],
            dst_ref=label_in.at[source],
            send_sem=label_send,
            recv_sem=label_recv,
            device_id={"sub": dest, "blk": blk},
            device_id_type=MESH,
        )

    pl.semaphore_wait(barrier, n_src - 1 + n_blk - 2)
    for dest in column[:-1]:
        label_copy(dest).start()
    label_in[source] = label_out[sub]
    for h in range(2):
        if h == 1:
            fill_slots(1)
        for dest in column[:-1]:
            slot_copy(dest, h).start()

        @pl.when(core != h)
        def _(h=h):
            slot_copy(sub, h).start()

        @pl.when(core == h)
        def _(h=h):
            slots_in[pl.ds(pl.multiple_of(source * width, width), width)] = slots_out[
                h, pl.ds(pl.multiple_of(sub * width, width), width)
            ]

    labels = label_in.at[pl.ds(0, n_sub - 1)]
    pltpu.make_async_copy(labels, labels, label_recv).wait()
    mine = label_in.at[pl.ds(core * n_sub, n_sub)]
    pair = pltpu.make_async_remote_copy(
        src_ref=mine,
        dst_ref=mine,
        send_sem=pair_send,
        recv_sem=pair_recv,
        device_id={"sub": sub, "blk": blk + 1 - 2 * core},
        device_id_type=MESH,
    )
    pair.start()
    pair.wait_recv()
    row_in = lax.broadcasted_iota(I32, (rows_owned * c8, LANES), 0) + 1
    for g in range(n_src // per_group):
        at = label_in[g * per_group]
        for s in range(1, per_group):
            at = at + label_in[g * per_group + s]
        pick[:, pl.ds(g * LANES, LANES)] = jnp.where(row_in == at, 1.0, 0.0).astype(BF16)
    blocks = slots_in.at[pl.ds(0, (n_src - 1) * width)]
    pltpu.make_async_copy(blocks, blocks, slot_recv).wait()
    sums_out[...] = jnp.dot(pick[...], slots_in[...], preferred_element_type=F32).astype(BF16)

    rows = rows_here * c8

    def send_sum(dest):
        pltpu.make_async_remote_copy(
            src_ref=sums_out.at[pl.ds(pl.multiple_of(dest * rows, rows), rows)],
            dst_ref=sums_in.at[core, chip],
            send_sem=sum_send,
            recv_sem=sum_recv.at[core],
            device_id={"sub": sub, "blk": dest},
            device_id_type=MESH,
        ).start()

    send_sum(blk + 1 - 2 * core)
    for other in plane:
        send_sum(other)
        send_sum(other + 1)
    keep = pltpu.make_async_copy(
        sums_out.at[pl.ds(pl.multiple_of(blk * rows, rows), rows)],
        sums_in.at[core, chip],
        sum_recv.at[core],
    )
    keep.start()
    pltpu.make_async_copy(labels, labels, label_send).wait()
    pltpu.make_async_copy(blocks, blocks, slot_send).wait()
    pair.wait_send()

    for h in range(2):
        pltpu.make_async_copy(sums_in.at[h], sums_in.at[h], sum_recv.at[h]).wait()
        acc = sums_in[h, 0].astype(F32)
        for j in range(1, n_chip):
            acc = acc + sums_in[h, j].astype(F32)
        for r in range(rows_here):
            for c in range(2):
                out_ref[pl.ds((r * 2 + c) * c8, c8), pl.ds(h * LANES, LANES)] = -acc[
                    r * c8 : (r + 1) * c8, c * LANES : (c + 1) * LANES
                ]
    sums = sums_out.at[pl.ds(0, (n_blk - 1) * rows)]
    pltpu.make_async_copy(sums, sums, sum_send).wait()


def on_device(inv_factor, coupling, batch_coupling, tile_rows, tile_count, row_place):
    n_sub, n_blk = lax.axis_size("sub"), lax.axis_size("blk")
    n_tiles, interior, dofs = coupling.shape[1:]
    cols = batch_coupling.shape[1] * batch_coupling.shape[2]
    c8 = cols // 2
    rows_here = row_place.shape[0] // (n_sub * n_blk)
    dims = (n_sub, n_blk, n_tiles, cols, rows_here)
    rows_owned = rows_here * n_blk
    slot_rows = n_sub * SLOTS * c8
    hbm = pl.BlockSpec(memory_space=pltpu.HBM)
    dma = pltpu.SemaphoreType.DMA
    out = pl.pallas_call(
        functools.partial(kernel, dims),
        out_shape=jax.ShapeDtypeStruct((rows_here * cols, dofs), F32),
        in_specs=[hbm] * 6,
        out_specs=pl.BlockSpec(memory_space=pltpu.VMEM),
        scratch_shapes=[
            pltpu.SMEM(tile_rows.shape, I32),
            pltpu.SMEM(tile_count.shape, I32),
            pltpu.SMEM(row_place.shape, I32),
            pltpu.VMEM((interior, interior), BF16),
            pltpu.VMEM((n_tiles, interior, dofs), BF16),
            pltpu.VMEM((cols, interior), BF16),
            pltpu.VMEM((n_tiles * c8, 2 * dofs), BF16),
            pltpu.VMEM((n_sub, 1, LANES), I32),
            pltpu.VMEM((2 * n_sub, 1, LANES), I32),
            pltpu.VMEM((2, slot_rows, dofs), BF16),
            pltpu.VMEM((2 * slot_rows, dofs), BF16),
            pltpu.VMEM((rows_owned * c8, 2 * slot_rows), BF16),
            pltpu.VMEM((rows_owned * c8, dofs), BF16),
            pltpu.VMEM((2, n_blk // 2, rows_here * c8, dofs), BF16),
            dma((6,)),
            dma,
            dma,
            dma,
            dma,
            dma,
            dma,
            dma,
            dma((2,)),
        ],
        compiler_params=pltpu.CompilerParams(
            collective_id=0, has_side_effects=True, vmem_limit_bytes=60 * 1024 * 1024
        ),
    )(
        tile_rows,
        tile_count,
        row_place,
        inv_factor[0],
        coupling[0],
        batch_coupling.reshape(cols, interior),
    )
    return out.reshape(rows_here, batch_coupling.shape[1], batch_coupling.shape[2], dofs)


def solution(mesh):
    return jax.shard_map(
        on_device,
        mesh=mesh,
        in_specs=(
            P(("sub", "blk"), None, None),
            P(("sub", "blk"), None, None, None),
            P(("sub", "blk"), None, None, None),
            P(("sub", "blk"), None),
            P(("sub", "blk")),
            P(),
        ),
        out_specs=P(("sub", "blk"), None, None, None),
        check_vma=False,
    )
```
